32 devices in a mesh: rep: 4 (over y, x), fsdp: 8 (over z, core).
Axes of the slice: x: 2, y: 2, z: 4, core: 2. Of those that a mesh axis runs over, the one named last changes fastest.
Arguments:
- residual_in: bfloat16 [8192, 2560], P(('rep', 'fsdp')), may hold values from -60 to 60
- mixed: bfloat16 [8192, 2560], P(('rep', 'fsdp')), may hold values from -6 to 6
- upstream: bfloat16 [8192, 2560], P(('rep', 'fsdp')), may hold values from -6 to 6
- norm_gain: float32 [2560], replicated, may hold values from 0.5 to 1.5
- weight: bfloat16 [4, 2560, 2560], P('rep', 'fsdp'), may hold values from -6 to 6
- momentum: float32 [4, 2560, 2560], P('rep', 'fsdp'), may hold values from -6 to 6
Outputs:
- input_grad: bfloat16 [8192, 2560], P(('rep', 'fsdp'))
- new_weight: bfloat16 [4, 2560, 2560], P('rep', 'fsdp')
- new_momentum: float32 [4, 2560, 2560], P('rep', 'fsdp')
The draws below stay inside these ranges and needn't reach their ends.
All inputs are finite; a program needn't handle non-finite values.
Results may differ from the reference program's by a relative error of at most 0.009.
Values may be sent and summed in bfloat16 or wider, within the bound.
No kernel may reach another device: no remote copies, remote signals or barrier semaphores. Data moves between devices by JAX's collectives and lax.ppermute only.
A program may use at most 128 MiB of HBM per device.

```python
import jax
import jax.numpy as jnp
import numpy as np
from jax import lax

D = 2560
TOK_DEV = 256
PARTNER_BIT = 1
TOKENS = 8192
N_REP = 4
N_FSDP = 8


def draw_residual_in(key, part):
    key = jax.random.fold_in(key, 11)
    key_base, key_rows, key_cols = jax.random.split(key, 3)
    row_scale = 10.0 ** jax.random.uniform(key_rows, (TOKENS, 1), jnp.float32, -0.5, 0.5)
    col_scale = 10.0 ** jax.random.uniform(key_cols, (1, D), jnp.float32, -0.5, 0.5)
    base = jax.random.truncated_normal(key_base, -6.0, 6.0, (TOKENS, D), jnp.float32)
    return (base * row_scale * col_scale).astype(jnp.bfloat16)


def with_spikes(values, rng, source, target, shards_of, factor):
    owner, partner = [(jnp.arange(values.shape[position]) // (values.shape[position] // shards_of)).reshape([-1 if axis == position else 1 for axis in range(values.ndim)]) for position in (source, target)]
    chosen = jax.random.permutation(rng, shards_of)[partner]
    strong = (owner == chosen) | (owner == (partner + shards_of // 2) % shards_of)
    return jnp.where(strong, factor * values, values)


def shard_levels(rng, dims, shards, least, largest):
    factor_of = 1.0
    for dim, blocks in shards:
        draws = jax.random.uniform(jax.random.fold_in(jax.random.fold_in(rng, 6), dim), (blocks,), jnp.float32, least / len(shards), largest / len(shards))
        factor_of = factor_of * jnp.repeat(jnp.exp(draws), dims[dim] // blocks).reshape((-1,) + (1,) * (len(dims) - 1 - dim))
    return factor_of


def noise(stream_key, shape, spread, most, shards=(), kind=jnp.bfloat16):
    values = jax.random.normal(stream_key, shape, jnp.float32) * spread
    if len(shards) > 0:
        values = shard_levels(stream_key, shape, shards, -0.22, 0.18) * values
    return jnp.clip(values, min=-most, max=most).astype(kind)


def noise_with(key, dims, spread, reach, shards, heavy, dtype=jnp.bfloat16):
    entries = spread * jax.random.normal(key, dims, jnp.float32)
    if shards:
        entries = entries * shard_levels(key, dims, shards, -0.22, 0.18)
    return jnp.clip(with_spikes(entries, jax.random.fold_in(key, 3), *heavy), -reach, reach).astype(dtype)


def setup_inputs(seed: int = 0) -> dict:
    arg_keys = jax.random.split(jax.random.key(seed), 7)
    return {
        "residual_in": draw_residual_in(jax.random.fold_in(arg_keys[6], 71), 0),
        "mixed": noise_with(arg_keys[1], (TOKENS, D), 1.0, 6.0, ((0, 32),), (0, 1, 32, 2.75)),
        "upstream": noise(arg_keys[2], (TOKENS, D), 1.0, 6.0, ((0, 32),)),
        "norm_gain": jnp.clip(1.0 + 0.1 * jax.random.normal(arg_keys[3], (D,), jnp.float32), 0.5, 1.5),
        "weight": noise(arg_keys[4], (N_REP, D, D), 1.0, 6.0, ((0, 4), (1, 8))),
        "momentum": noise(arg_keys[5], (N_REP, D, D), 1.0, 6.0, ((0, 4), (1, 8)), jnp.float32),
    }


EPSILON = 1e-05
LEARN_RATE = 0.05
MOMENTUM_DECAY = 0.9

def group_update(resid, mixed_rows, cot_rows, norm_gain, weight_one, moment_one):
    weight_scale = D ** (-0.5)
    projected = jnp.dot(mixed_rows, weight_one, preferred_element_type=jnp.float32) * weight_scale
    summed = resid.astype(jnp.float32) + projected
    inv_rms = lax.rsqrt(lax.optimization_barrier(jnp.mean(summed * summed, axis=-1, keepdims=True)) + EPSILON)
    scaled_cot = cot_rows.astype(jnp.float32) * norm_gain
    inner = lax.optimization_barrier(jnp.mean(scaled_cot * summed, axis=-1, keepdims=True))
    cot_summed = (inv_rms * (scaled_cot - summed * inner * inv_rms * inv_rms)).astype(jnp.bfloat16)
    input_grad = (jnp.dot(cot_summed, weight_one.T, preferred_element_type=jnp.float32) * weight_scale).astype(jnp.bfloat16)
    mixed_blocks = mixed_rows.reshape(N_FSDP, TOK_DEV, D)
    cot_blocks = cot_summed.reshape(N_FSDP, TOK_DEV, D)

    def add_block(carried, pair):
        term = lax.dot_general(pair[0], pair[1], (((0,), (0,)), ((), ())), preferred_element_type=jnp.float32) * weight_scale
        term = lax.optimization_barrier(term.astype(jnp.bfloat16)).astype(jnp.float32)
        return (carried + term, None)
    gradient, unused = lax.scan(add_block, jnp.zeros((D, D), jnp.float32), (mixed_blocks, cot_blocks))
    moment_next = MOMENTUM_DECAY * moment_one + gradient
    weight_next = (weight_one.astype(jnp.float32) - LEARN_RATE * moment_next).astype(jnp.bfloat16)
    return (input_grad, weight_next, moment_next)

def reference(residual_in, mixed, upstream, norm_gain, weight, momentum):
    group_rows = TOK_DEV * N_FSDP
    grads_in = []
    weights_next = []
    moments_next = []
    for group in range(N_REP):
        lower = group * group_rows
        result = group_update(residual_in[lower:lower + group_rows], mixed[lower:lower + group_rows], upstream[lower:lower + group_rows], norm_gain, weight[group], momentum[group])
        grads_in.append(result[0])
        weights_next.append(result[1])
        moments_next.append(result[2])
    input_grad = jnp.concatenate(grads_in, axis=0)
    weight_next = jnp.stack(weights_next)
    moment_next = jnp.stack(moments_next)
    partner = np.arange(N_REP) ^ 1 << PARTNER_BIT
    new_weight = ((weight_next.astype(jnp.float32) + weight_next[partner].astype(jnp.float32)) * 0.5).astype(jnp.bfloat16)
    new_momentum = (moment_next + moment_next[partner]) * 0.5
    return (input_grad, new_weight, new_momentum)
```

```python
import functools

import jax
import jax.numpy as jnp
from jax import lax
from jax.experimental import pallas as pl
from jax.experimental.pallas import tpu as pltpu
from jax.sharding import PartitionSpec as P

PARTNER_BIT = 1

EPSILON = 1e-05
LEARN_RATE = 0.05
MOMENTUM_DECAY = 0.9

FWD_CHUNKS = 4
BWD_CHUNKS = 4
COST_SHARE = 0.01
BF = jnp.bfloat16
F32 = jnp.float32


def params(mib=48):
    return pltpu.CompilerParams(vmem_limit_bytes=mib << 20)


def cost(flops, moved):
    return pl.CostEstimate(
        flops=int(flops * COST_SHARE), bytes_accessed=int(moved * COST_SHARE), transcendentals=0
    )


def whole():
    return pl.BlockSpec(memory_space=pltpu.VMEM)


def after(block, *others):
    return lax.optimization_barrier((block, *others))[0]


def from_partner(block):
    count = lax.axis_size("rep")
    return lax.ppermute(block, "rep", [(g, g ^ (1 << PARTNER_BIT)) for g in range(count)])


def from_mate(block, bit):
    count = lax.axis_size("fsdp")
    return lax.ppermute(block, "fsdp", [(f, f ^ bit) for f in range(count)])


def shift_far(block, hops):
    count = lax.axis_size("fsdp")
    return lax.ppermute(block, "fsdp", [(f, (f + 4 * hops) % count) for f in range(count)])


def forward_kernel(scale, rows, n_far, place, x_ref, own_ref, mate_ref, *refs):
    fars, rest = refs[: 2 * n_far], refs[2 * n_far :]
    w_ref, keep_ref, give_ref = rest
    for i, ref in enumerate((own_ref, mate_ref, *fars)):
        w_ref[pl.ds(pl.multiple_of(place[i] * rows, 16), rows), :] = ref[...]
    part = jnp.dot(x_ref[...], w_ref[...], preferred_element_type=F32) * scale
    tokens = keep_ref.shape[0]
    keep_ref[...] = part[:tokens]
    give_ref[...] = part[tokens:].astype(BF)


def forward_part(place, x, own, mate, fars, chunk, width, scale):
    tokens, depth = x.shape[0] // 2, x.shape[1]
    rows = own.shape[0]
    column = pl.BlockSpec((rows, width), lambda i, place: (0, chunk))
    full = lambda shape: pl.BlockSpec(shape, lambda i, place: (0, 0))
    return pl.pallas_call(
        functools.partial(forward_kernel, scale, rows, len(fars) // 2),
        grid_spec=pltpu.PrefetchScalarGridSpec(
            num_scalar_prefetch=1,
            grid=(1,),
            in_specs=[full(x.shape), column, column] + [full(w.shape) for w in fars],
            out_specs=[full((depth, width)), full((tokens, width)), full((tokens, width))],
        ),
        out_shape=[
            jax.ShapeDtypeStruct((depth, width), BF),
            jax.ShapeDtypeStruct((tokens, width), F32),
            jax.ShapeDtypeStruct((tokens, width), BF),
        ],
        compiler_params=params(),
        cost_estimate=cost(4 * tokens * depth * width, 2 * depth * (2 * width + 2 * tokens)),
        name="forward_part",
    )(place, x, own, mate, *fars)


def norm_kernel(n_in, n_out, res_ref, up_ref, gain_ref, *refs):
    keeps, gots, cots = refs[:n_in], refs[n_in : 2 * n_in], refs[2 * n_in :]
    width = keeps[0].shape[1]
    features = n_in * width
    summed, scaled = [], []
    square = inner = 0.0
    for i in range(n_in):
        cols = slice(i * width, (i + 1) * width)
        s = res_ref[:, cols].astype(F32) + (keeps[i][...] + gots[i][...].astype(F32))
        c = up_ref[:, cols].astype(F32) * gain_ref[:, cols]
        square += jnp.sum(s * s, axis=-1, keepdims=True)
        inner += jnp.sum(c * s, axis=-1, keepdims=True)
        summed.append(s)
        scaled.append(c)
    inv_rms = lax.rsqrt(square / features + EPSILON)
    pull = inner / features * inv_rms * inv_rms
    out_width = cots[0].shape[1]
    for i in range(n_in):
        cot = (inv_rms * (scaled[i] - summed[i] * pull)).astype(BF)
        if n_in == n_out:
            cots[i][...] = cot
        else:
            start = i * width
            at = start
            while at < start + width:
                j = at // out_width
                end = min((j + 1) * out_width, start + width)
                cots[j][:, at - j * out_width : end - j * out_width] = cot[:, at - start : end - start]
                at = end


def norm_cot(residual, upstream, gain, keeps, gots, n_out):
    tokens, features = residual.shape
    tile = 64
    n_in = len(keeps)
    width, out_width = features // n_in, features // n_out
    row = lambda w: pl.BlockSpec((tile, w), lambda i: (i, 0))
    return pl.pallas_call(
        functools.partial(norm_kernel, n_in, n_out),
        grid=(tokens // tile,),
        in_specs=[row(features), row(features), pl.BlockSpec((1, features), lambda i: (0, 0))]
        + [row(width)] * (2 * n_in),
        out_specs=[row(out_width)] * n_out,
        out_shape=[jax.ShapeDtypeStruct((tokens, out_width), BF)] * n_out,
        compiler_params=params(),
        cost_estimate=cost(20 * tokens * features, 12 * tokens * features),
        name="norm_cot",
    )(residual, upstream, gain.reshape(1, features), *keeps, *gots)


def gradient_kernel(scale, x_ref, *refs):
    cots, (keep_ref, give_ref) = refs[:4], refs[4:]
    cot = jnp.concatenate([ref[...] for ref in cots], axis=0)
    part = jnp.dot(x_ref[...], cot, preferred_element_type=F32) * scale
    half = keep_ref.shape[0]
    keep_ref[...] = part[:half]
    give_ref[...] = part[half:].astype(BF)


def gradient_part(x_rows, cots, scale):
    rows, tokens = x_rows.shape
    width = cots[0].shape[1]
    return pl.pallas_call(
        functools.partial(gradient_kernel, scale),
        in_specs=[whole()] * 5,
        out_specs=[whole()] * 2,
        out_shape=[
            jax.ShapeDtypeStruct((rows // 2, width), F32),
            jax.ShapeDtypeStruct((rows // 2, width), BF),
        ],
        compiler_params=params(),
        cost_estimate=cost(2 * rows * tokens * width, 2 * tokens * (rows + width) + 3 * rows * width),
        name="gradient_part",
    )(x_rows, *cots)


def input_grad_kernel(scale, n_cot, n_weight, *refs):
    own, nb = refs[:n_cot], refs[n_cot : 2 * n_cot]
    weights = refs[2 * n_cot : 2 * n_cot + n_weight]
    keep_ref, give_ref = refs[2 * n_cot + n_weight :]
    cot = jnp.concatenate(
        [jnp.concatenate([ref[...] for ref in side], axis=1) for side in (own, nb)], axis=0
    )
    width = weights[0].shape[1]
    total = 0.0
    for i, ref in enumerate(weights):
        total += lax.dot_general(
            cot[:, i * width : (i + 1) * width],
            ref[...],
            (((1,), (1,)), ((), ())),
            preferred_element_type=F32,
        )
    total = (total * scale).astype(BF)
    tokens = keep_ref.shape[0]
    keep_ref[...] = total[:tokens]
    give_ref[...] = total[tokens:]


def input_grad_part(own, nb, weights, scale):
    tokens = own[0].shape[0]
    depth = weights[0].shape[0]
    features = len(weights) * weights[0].shape[1]
    count = 2 * len(own) + len(weights)
    return pl.pallas_call(
        functools.partial(input_grad_kernel, scale, len(own), len(weights)),
        in_specs=[whole()] * count,
        out_specs=[whole()] * 2,
        out_shape=[jax.ShapeDtypeStruct((tokens, depth), BF)] * 2,
        compiler_params=params(),
        cost_estimate=cost(
            4 * tokens * depth * features, 2 * depth * features + 4 * tokens * (depth + features)
        ),
        name="input_grad_part",
    )(*own, *nb, *weights)


def split_kernel(n_quad, near, mixed_ref, own_ref, give_ref):
    width = own_ref.shape[1] // n_quad
    for side in range(2):

        @pl.when(near[0] == side)
        def _():
            for i in range(n_quad):
                to = slice(i * width, (i + 1) * width)
                ours, theirs = 2 * i + side, 2 * i + 1 - side
                own_ref[:, to] = mixed_ref[:, ours * width : (ours + 1) * width]
                give_ref[:, to] = mixed_ref[:, theirs * width : (theirs + 1) * width]


def split(near, mixed, n_quad):
    tokens, features = mixed.shape
    tile = 64
    row = lambda w: pl.BlockSpec((tile, w), lambda i, near: (i, 0))
    return pl.pallas_call(
        functools.partial(split_kernel, n_quad),
        grid_spec=pltpu.PrefetchScalarGridSpec(
            num_scalar_prefetch=1,
            grid=(tokens // tile,),
            in_specs=[row(features)],
            out_specs=[row(features // 2)] * 2,
        ),
        out_shape=[jax.ShapeDtypeStruct((tokens, features // 2), BF)] * 2,
        compiler_params=params(),
        cost_estimate=cost(0, 4 * tokens * features),
        name="split",
    )(near, mixed)


def interleave_kernel(n_quad, near, own_ref, got_ref, out_ref):
    width = own_ref.shape[1] // n_quad
    for side in range(2):

        @pl.when(near[0] == side)
        def _():
            for i in range(n_quad):
                at = slice(i * width, (i + 1) * width)
                ours, theirs = 2 * i + side, 2 * i + 1 - side
                out_ref[:, ours * width : (ours + 1) * width] = own_ref[:, at]
                out_ref[:, theirs * width : (theirs + 1) * width] = got_ref[:, at]


def interleave(near, own, got, n_quad):
    tokens, depth = own.shape
    tile = 64
    row = lambda w: pl.BlockSpec((tile, w), lambda i, near: (i, 0))
    return pl.pallas_call(
        functools.partial(interleave_kernel, n_quad),
        grid_spec=pltpu.PrefetchScalarGridSpec(
            num_scalar_prefetch=1,
            grid=(tokens // tile,),
            in_specs=[row(depth)] * 2,
            out_specs=row(2 * depth),
        ),
        out_shape=jax.ShapeDtypeStruct((tokens, 2 * depth), BF),
        compiler_params=params(),
        cost_estimate=cost(0, 8 * tokens * depth),
        name="interleave",
    )(near, own, got)


def update_kernel(count, place, w_ref, pw_ref, m_ref, pm_ref, *refs):
    ours, theirs = refs[:count], refs[count : 2 * count]
    weight_ref, moment_ref = refs[2 * count :]
    mine = pl.program_id(0) == 0
    width = ours[0].shape[1]
    for i in range(count):
        cols = slice(i * width, (i + 1) * width)
        grads = jnp.where(mine, ours[i][...], theirs[i][...].astype(F32))
        moment = 0.5 * (
            MOMENTUM_DECAY * (m_ref[0, :, cols] + pm_ref[:, cols].astype(F32)) + grads
        )
        moment_ref[0, :, cols] = moment
        both = w_ref[0, :, cols].astype(F32) + pw_ref[:, cols].astype(F32)
        weight_ref[0, :, cols] = (0.5 * both - LEARN_RATE * moment).astype(BF)


def update(side, weight, partner_weight, momentum, partner_moment, ours, theirs):
    _, rows, features = weight.shape
    half = rows // 2
    width = ours[0].shape[1]
    block3 = pl.BlockSpec((1, half, features), lambda i, side: (0, (side[0] + i) % 2, 0))
    block2 = pl.BlockSpec((half, features), lambda i, side: ((side[0] + i) % 2, 0))
    fixed = pl.BlockSpec((half, width), lambda i, side: (0, 0))
    return pl.pallas_call(
        functools.partial(update_kernel, len(ours)),
        grid_spec=pltpu.PrefetchScalarGridSpec(
            num_scalar_prefetch=1,
            grid=(2,),
            in_specs=[block3, block2, block3, block2] + [fixed] * (2 * len(ours)),
            out_specs=[block3, block3],
        ),
        out_shape=[
            jax.ShapeDtypeStruct(weight.shape, BF),
            jax.ShapeDtypeStruct(momentum.shape, F32),
        ],
        compiler_params=params(),
        cost_estimate=cost(10 * rows * features, 18 * rows * features),
        name="update",
    )(side, weight, partner_weight, momentum, partner_moment, *ours, *theirs)


def per_device(residual_in, mixed, upstream, norm_gain, weight, momentum):
    tokens, features = mixed.shape
    scale = features ** (-0.5)
    count = lax.axis_size("fsdp")
    n_quad = count // 4
    rows = weight.shape[1]
    me = lax.axis_index("fsdp")
    quad, core, near = me // 4, me % 2, (me // 2) % 2
    side = (lax.axis_index("rep") >> PARTNER_BIT) & 1
    own = weight[0]

    width = features // FWD_CHUNKS
    cols = [slice(i * width, (i + 1) * width) for i in range(FWD_CHUNKS)]
    x_own, x_give = split(near.reshape(1).astype(jnp.int32), mixed, n_quad)
    x_nb = from_mate(x_give, 2)
    fars = [[shift_far(own[:, c], d) for d in range(1, n_quad)] for c in cols]
    mate = from_mate(own, 1)
    partner_weight = from_partner(own)
    partner_moment = from_partner(momentum[0].astype(BF))

    quads = [quad] + [(quad + n_quad - d) % n_quad for d in range(1, n_quad)]
    place = jnp.stack(
        [quads[0] * 2 + core, quads[0] * 2 + 1 - core]
        + [q * 2 + core for q in quads[1:]]
        + [q * 2 + 1 - core for q in quads[1:]]
    ).astype(jnp.int32)

    x = jnp.concatenate([x_own, x_nb], axis=0)
    on = [(quad + d) % n_quad for d in range(n_quad)]
    block = lambda q, c: lax.dynamic_slice(x, (0, (q * 2 + c) * rows), (2 * tokens, rows))
    x_mine = jnp.concatenate([block(q, core) for q in on], axis=1)
    x_theirs = from_mate(jnp.concatenate([block(q, 1 - core) for q in on], axis=1), 1)
    x_rows = jnp.concatenate([x_mine, x_theirs], axis=0).T.reshape(n_quad, 2, rows // 2, 4 * tokens)
    x_rows = jnp.where(side == 0, x_rows, x_rows[:, ::-1])
    x_rows = jnp.swapaxes(x_rows, 0, 1).reshape(n_quad * rows, 4 * tokens)

    weights, keeps, gots = [], [], []
    for i in range(FWD_CHUNKS):
        seen = [partner_weight] if i == 2 else [x_rows, partner_moment] if i == 3 else []
        seen += gots[i - 2 : i - 1] if i > 1 else []
        seen += keeps[-1:]
        far_mates = [from_mate(after(w, *seen), 1) for w in fars[i]]
        w_rows, keep, give = forward_part(place, x, own, mate, fars[i] + far_mates, i, width, scale)
        weights.append(w_rows)
        keeps.append(keep)
        gots.append(from_mate(give, 2))

    keeps[0] = after(keeps[0], partner_weight, partner_moment, x_rows)
    cots = list(norm_cot(residual_in, upstream, norm_gain, keeps, gots, BWD_CHUNKS))

    half = rows // 2
    nbs = [from_mate(cot, 2) for cot in cots]
    mates = [from_mate(cot, 1) for cot in cots]
    kept, got, ours, theirs = [], [], [], []

    def gather(i):
        both = kept[i] + got[i].astype(F32)
        total = both[:half]
        for d in range(1, n_quad):
            total += shift_far(both[d * half : (d + 1) * half].astype(BF), d).astype(F32)
        ours.append(total)
        theirs.append(from_partner(total.astype(BF)))

    far_sums = []

    def sum_far(i):
        both = kept[i] + got[i].astype(F32)
        far_sums.append(
            [shift_far(both[d * half : (d + 1) * half].astype(BF), d) for d in range(1, n_quad)]
        )
        ours.append(both[:half])

    def give_back(i):
        for block in far_sums[i]:
            ours[i] += block.astype(F32)
        theirs.append(from_partner(ours[i].astype(BF)))

    nb_mates = []
    for i in range(BWD_CHUNKS):
        nb_mates.append(from_mate(nbs[i], 1))
    for i in range(BWD_CHUNKS + 2):
        if i < BWD_CHUNKS:
            seen = got[-1:] + (far_sums[-1] if far_sums else []) + theirs[-1:]
            seen += nb_mates[i + 1 : i + 2] if i else []
            keep, give = gradient_part(
                after(x_rows, *seen) if seen else x_rows, [cots[i], nbs[i], mates[i], nb_mates[i]], scale
            )
            kept.append(keep)
        if 0 <= i - 2:
            give_back(i - 2)
        if 0 <= i - 1 < BWD_CHUNKS:
            sum_far(i - 1)
        if i < BWD_CHUNKS:
            got.append(from_partner(give))

    ig_own, ig_nb = input_grad_part([after(cots[0], kept[-1])] + cots[1:], nbs, weights, scale)
    ig_got = from_mate(ig_nb, 2)
    input_grad = interleave(near.reshape(1).astype(jnp.int32), ig_own, ig_got, n_quad)

    new_weight, new_momentum = update(
        side.reshape(1).astype(jnp.int32), weight, partner_weight, momentum, partner_moment, ours, theirs
    )
    return (input_grad, new_weight, new_momentum)


def solution(mesh):
    return jax.shard_map(
        per_device,
        mesh=mesh,
        in_specs=(
            P(("rep", "fsdp"), None),
            P(("rep", "fsdp"), None),
            P(("rep", "fsdp"), None),
            P(),
            P("rep", "fsdp", None),
            P("rep", "fsdp", None),
        ),
        out_specs=(P(("rep", "fsdp"), None), P("rep", "fsdp", None), P("rep", "fsdp", None)),
        check_vma=False,
    )
```

```python
import functools

import jax
import jax.numpy as jnp
from jax import lax
from jax.experimental import pallas as pl
from jax.experimental.pallas import tpu as pltpu
from jax.sharding import PartitionSpec as P

PARTNER_BIT = 1

EPSILON = 1e-05
LEARN_RATE = 0.05
MOMENTUM_DECAY = 0.9

FWD_PARTS = (8, 8, 4)
BWD_PARTS = (8, 8, 4)
IN_FLIGHT = 1
COST_SHARE = 0.01
BF = jnp.bfloat16
F32 = jnp.float32


def params(mib=48):
    return pltpu.CompilerParams(vmem_limit_bytes=mib << 20)


def cost(flops, moved):
    return pl.CostEstimate(
        flops=int(flops * COST_SHARE), bytes_accessed=int(moved * COST_SHARE), transcendentals=0
    )


def whole():
    return pl.BlockSpec(memory_space=pltpu.VMEM)


def after(block, *others):
    return lax.optimization_barrier((block, *others))[0]


def from_partner(block):
    count = lax.axis_size("rep")
    return lax.ppermute(block, "rep", [(g, g ^ (1 << PARTNER_BIT)) for g in range(count)])


def from_mate(block, bit):
    count = lax.axis_size("fsdp")
    return lax.ppermute(block, "fsdp", [(f, f ^ bit) for f in range(count)])


def shift_far(block, hops):
    count = lax.axis_size("fsdp")
    return lax.ppermute(block, "fsdp", [(f, (f + 4 * hops) % count) for f in range(count)])


def chunks(parts, features):
    unit = features // sum(parts)
    return [(sum(parts[:i]) * unit, part * unit) for i, part in enumerate(parts)]


def put_rows(place, rows, refs, w_ref, start):
    for i, ref in enumerate(refs):
        at = pl.ds(pl.multiple_of(place[i] * rows, 16), rows)
        w_ref[at, start : start + ref.shape[1]] = ref[...]


def forward_kernel(scale, rows, place, x_ref, *refs):
    pieces, (keep_ref, give_ref, w_ref) = refs[:-3], refs[-3:]
    put_rows(place, rows, pieces, w_ref, 0)
    part = jnp.dot(x_ref[...], w_ref[...], preferred_element_type=F32) * scale
    tokens = keep_ref.shape[0]
    keep_ref[...] = part[:tokens]
    give_ref[...] = part[tokens:].astype(BF)


def forward_part(place, x, own, mate, fars, start, width, scale):
    tokens, depth = x.shape[0] // 2, x.shape[1]
    rows = own.shape[0]
    column = pl.BlockSpec((rows, width), lambda i, place: (0, start // width))
    full = lambda shape: pl.BlockSpec(shape, lambda i, place: (0, 0))
    return pl.pallas_call(
        functools.partial(forward_kernel, scale, rows),
        grid_spec=pltpu.PrefetchScalarGridSpec(
            num_scalar_prefetch=1,
            grid=(1,),
            in_specs=[full(x.shape), column, column] + [full(w.shape) for w in fars],
            out_specs=[full((tokens, width)), full((tokens, width))],
            scratch_shapes=[pltpu.VMEM((depth, width), BF)],
        ),
        out_shape=[
            jax.ShapeDtypeStruct((tokens, width), F32),
            jax.ShapeDtypeStruct((tokens, width), BF),
        ],
        compiler_params=params(),
        cost_estimate=cost(4 * tokens * depth * width, 2 * depth * (2 * width + 2 * tokens)),
        name="forward_part",
    )(place, x, own, mate, *fars)


def norm_kernel(n_in, n_out, res_ref, up_ref, gain_ref, *refs):
    keeps, gots, cots = refs[:n_in], refs[n_in : 2 * n_in], refs[2 * n_in :]
    features = res_ref.shape[1]
    summed, scaled = [], []
    square = inner = 0.0
    start = 0
    for keep, got in zip(keeps, gots):
        cols = slice(start, start + keep.shape[1])
        start = cols.stop
        s = res_ref[:, cols].astype(F32) + (keep[...] + got[...].astype(F32))
        c = up_ref[:, cols].astype(F32) * gain_ref[:, cols]
        square += jnp.sum(s * s, axis=-1, keepdims=True)
        inner += jnp.sum(c * s, axis=-1, keepdims=True)
        summed.append(s)
        scaled.append(c)
    inv_rms = lax.rsqrt(square / features + EPSILON)
    pull = inner / features * inv_rms * inv_rms
    start = 0
    for s, c in zip(summed, scaled):
        cot = (inv_rms * (c - s * pull)).astype(BF)
        end = start + s.shape[1]
        first = 0
        for ref in cots:
            last = first + ref.shape[1]
            low, high = max(first, start), min(last, end)
            if low < high:
                ref[:, low - first : high - first] = cot[:, low - start : high - start]
            first = last
        start = end


def norm_cot(residual, upstream, gain, keeps, gots, widths):
    tokens, features = residual.shape
    tile = 64
    row = lambda w: pl.BlockSpec((tile, w), lambda i: (i, 0))
    return pl.pallas_call(
        functools.partial(norm_kernel, len(keeps), len(widths)),
        grid=(tokens // tile,),
        in_specs=[row(features), row(features), pl.BlockSpec((1, features), lambda i: (0, 0))]
        + [row(keep.shape[1]) for keep in keeps] * 2,
        out_specs=[row(w) for w in widths],
        out_shape=[jax.ShapeDtypeStruct((tokens, w), BF) for w in widths],
        compiler_params=params(),
        cost_estimate=cost(20 * tokens * features, 12 * tokens * features),
        name="norm_cot",
    )(residual, upstream, gain.reshape(1, features), *keeps, *gots)


def gradient_kernel(scale, x_ref, *refs):
    cots, (keep_ref, give_ref) = refs[:4], refs[4:]
    cot = jnp.concatenate([ref[...] for ref in cots], axis=0)
    part = jnp.dot(x_ref[...], cot, preferred_element_type=F32) * scale
    half = keep_ref.shape[0]
    keep_ref[...] = part[:half]
    give_ref[...] = part[half:].astype(BF)


def gradient_part(x_rows, cots, scale):
    rows, tokens = x_rows.shape
    width = cots[0].shape[1]
    return pl.pallas_call(
        functools.partial(gradient_kernel, scale),
        in_specs=[whole()] * 5,
        out_specs=[whole()] * 2,
        out_shape=[
            jax.ShapeDtypeStruct((rows // 2, width), F32),
            jax.ShapeDtypeStruct((rows // 2, width), BF),
        ],
        compiler_params=params(),
        cost_estimate=cost(2 * rows * tokens * width, 2 * tokens * (rows + width) + 3 * rows * width),
        name="gradient_part",
    )(x_rows, *cots)


def input_grad_kernel(scale, rows, n_cot, place, own_ref, mate_ref, *refs):
    own, nb = refs[:n_cot], refs[n_cot : 2 * n_cot]
    fars, (keep_ref, give_ref, w_ref) = refs[2 * n_cot : -3], refs[-3:]
    put_rows(place, rows, (own_ref, mate_ref), w_ref, 0)
    each = w_ref.shape[0] // rows - 2
    start = 0
    for i in range(0, len(fars), each):
        for n, ref in enumerate(fars[i : i + each]):
            at = pl.ds(pl.multiple_of(place[2 + n] * rows, 16), rows)
            w_ref[at, start : start + ref.shape[1]] = ref[...]
        start += fars[i].shape[1]
    tokens = keep_ref.shape[0]
    for cots, out_ref in ((nb, give_ref), (own, keep_ref)):
        cot = jnp.concatenate([ref[...] for ref in cots], axis=1)
        total = lax.dot_general(
            cot, w_ref[...], (((1,), (1,)), ((), ())), preferred_element_type=F32
        )
        out_ref[...] = (total * scale).astype(BF)


def input_grad_part(place, own, mate, own_cots, nb_cots, fars, scale):
    tokens = own_cots[0].shape[0]
    rows, features = own.shape
    depth = rows * (2 + len(fars[0]))
    flat = [w for chunk in fars for w in chunk]
    operands = [own, mate, *own_cots, *nb_cots, *flat]
    full = lambda shape: pl.BlockSpec(shape, lambda i, place: (0, 0))
    return pl.pallas_call(
        functools.partial(input_grad_kernel, scale, rows, len(own_cots)),
        grid_spec=pltpu.PrefetchScalarGridSpec(
            num_scalar_prefetch=1,
            grid=(1,),
            in_specs=[full(a.shape) for a in operands],
            out_specs=[full((tokens, depth))] * 2,
            scratch_shapes=[pltpu.VMEM((depth, features), BF)],
        ),
        out_shape=[jax.ShapeDtypeStruct((tokens, depth), BF)] * 2,
        compiler_params=params(),
        cost_estimate=cost(
            4 * tokens * depth * features, 2 * depth * features + 4 * tokens * (depth + features)
        ),
        name="input_grad_part",
    )(place, *operands)


def split_kernel(n_quad, near, mixed_ref, own_ref, give_ref):
    width = own_ref.shape[1] // n_quad
    for side in range(2):

        @pl.when(near[0] == side)
        def _():
            for i in range(n_quad):
                to = slice(i * width, (i + 1) * width)
                ours, theirs = 2 * i + side, 2 * i + 1 - side
                own_ref[:, to] = mixed_ref[:, ours * width : (ours + 1) * width]
                give_ref[:, to] = mixed_ref[:, theirs * width : (theirs + 1) * width]


def split(near, mixed, n_quad):
    tokens, features = mixed.shape
    tile = 64
    row = lambda w: pl.BlockSpec((tile, w), lambda i, near: (i, 0))
    return pl.pallas_call(
        functools.partial(split_kernel, n_quad),
        grid_spec=pltpu.PrefetchScalarGridSpec(
            num_scalar_prefetch=1,
            grid=(tokens // tile,),
            in_specs=[row(features)],
            out_specs=[row(features // 2)] * 2,
        ),
        out_shape=[jax.ShapeDtypeStruct((tokens, features // 2), BF)] * 2,
        compiler_params=params(),
        cost_estimate=cost(0, 4 * tokens * features),
        name="split",
    )(near, mixed)


def interleave_kernel(n_quad, near, own_ref, got_ref, out_ref):
    width = own_ref.shape[1] // n_quad
    for side in range(2):

        @pl.when(near[0] == side)
        def _():
            for i in range(n_quad):
                at = slice(i * width, (i + 1) * width)
                ours, theirs = 2 * i + side, 2 * i + 1 - side
                out_ref[:, ours * width : (ours + 1) * width] = own_ref[:, at]
                out_ref[:, theirs * width : (theirs + 1) * width] = got_ref[:, at]


def interleave(near, own, got, n_quad):
    tokens, depth = own.shape
    tile = 64
    row = lambda w: pl.BlockSpec((tile, w), lambda i, near: (i, 0))
    return pl.pallas_call(
        functools.partial(interleave_kernel, n_quad),
        grid_spec=pltpu.PrefetchScalarGridSpec(
            num_scalar_prefetch=1,
            grid=(tokens // tile,),
            in_specs=[row(depth)] * 2,
            out_specs=row(2 * depth),
        ),
        out_shape=jax.ShapeDtypeStruct((tokens, 2 * depth), BF),
        compiler_params=params(),
        cost_estimate=cost(0, 8 * tokens * depth),
        name="interleave",
    )(near, own, got)


def update_kernel(count, place, w_ref, pw_ref, m_ref, pm_ref, *refs):
    ours, theirs = refs[:count], refs[count : 2 * count]
    weight_ref, moment_ref = refs[2 * count :]
    mine = pl.program_id(0) == 0
    start = 0
    for i in range(count):
        cols = slice(start, start + ours[i].shape[1])
        start = cols.stop
        grads = jnp.where(mine, ours[i][...], theirs[i][...].astype(F32))
        moment = 0.5 * (
            MOMENTUM_DECAY * (m_ref[0, :, cols] + pm_ref[:, cols].astype(F32)) + grads
        )
        moment_ref[0, :, cols] = moment
        both = w_ref[0, :, cols].astype(F32) + pw_ref[:, cols].astype(F32)
        weight_ref[0, :, cols] = (0.5 * both - LEARN_RATE * moment).astype(BF)


def update(side, weight, partner_weight, momentum, partner_moment, ours, theirs):
    _, rows, features = weight.shape
    half = rows // 2
    block3 = pl.BlockSpec((1, half, features), lambda i, side: (0, (side[0] + i) % 2, 0))
    block2 = pl.BlockSpec((half, features), lambda i, side: ((side[0] + i) % 2, 0))
    fixed = [pl.BlockSpec(block.shape, lambda i, side: (0, 0)) for block in ours]
    return pl.pallas_call(
        functools.partial(update_kernel, len(ours)),
        grid_spec=pltpu.PrefetchScalarGridSpec(
            num_scalar_prefetch=1,
            grid=(2,),
            in_specs=[block3, block2, block3, block2] + fixed * 2,
            out_specs=[block3, block3],
        ),
        out_shape=[
            jax.ShapeDtypeStruct(weight.shape, BF),
            jax.ShapeDtypeStruct(momentum.shape, F32),
        ],
        compiler_params=params(),
        cost_estimate=cost(10 * rows * features, 18 * rows * features),
        name="update",
    )(side, weight, partner_weight, momentum, partner_moment, *ours, *theirs)


def per_device(residual_in, mixed, upstream, norm_gain, weight, momentum):
    tokens, features = mixed.shape
    scale = features ** (-0.5)
    count = lax.axis_size("fsdp")
    n_quad = count // 4
    rows = weight.shape[1]
    me = lax.axis_index("fsdp")
    quad, core, near = me // 4, me % 2, (me // 2) % 2
    side = (lax.axis_index("rep") >> PARTNER_BIT) & 1
    own = weight[0]

    cols = chunks(FWD_PARTS, features)
    slices = [own[:, start : start + width] for start, width in cols]
    fars = []
    for i, piece in enumerate(slices):
        if i >= IN_FLIGHT:
            piece = after(piece, *fars[i - IN_FLIGHT])
        fars.append([shift_far(piece, d) for d in range(1, n_quad)])
    x_own, x_give = split(near.reshape(1).astype(jnp.int32), after(mixed, *slices), n_quad)
    x_nb = from_mate(x_give, 2)
    mate = from_mate(own, 1)
    partner_weight = from_partner(own)
    partner_moment = from_partner(momentum[0].astype(BF))

    quads = [quad] + [(quad + n_quad - d) % n_quad for d in range(1, n_quad)]
    place = jnp.stack(
        [quads[0] * 2 + core, quads[0] * 2 + 1 - core]
        + [q * 2 + core for q in quads[1:]]
        + [q * 2 + 1 - core for q in quads[1:]]
    ).astype(jnp.int32)

    x = jnp.concatenate([x_own, x_nb], axis=0)
    on = [(quad + d) % n_quad for d in range(n_quad)]
    block = lambda q, c: lax.dynamic_slice(x, (0, (q * 2 + c) * rows), (2 * tokens, rows))
    x_mine = jnp.concatenate([block(q, core) for q in on], axis=1)
    x_theirs = from_mate(jnp.concatenate([block(q, 1 - core) for q in on], axis=1), 1)
    x_rows = jnp.concatenate([x_mine, x_theirs], axis=0).T.reshape(n_quad, 2, rows // 2, 4 * tokens)
    x_rows = jnp.where(side == 0, x_rows, x_rows[:, ::-1])
    x_rows = jnp.swapaxes(x_rows, 0, 1).reshape(n_quad * rows, 4 * tokens)

    pieces, keeps, gots = [], [], []
    for i, (start, width) in enumerate(cols):
        seen = keeps[-1:]
        if i == len(cols) - 1:
            seen += gots[:-1] + [x_rows, partner_weight]
        far_mates = [from_mate(after(w, *seen) if seen else w, 1) for w in fars[i]]
        pieces.append(fars[i] + far_mates)
        keep, give = forward_part(place, x, own, mate, pieces[i], start, width, scale)
        keeps.append(keep)
        gots.append(from_mate(give, 2))

    keeps[0] = after(keeps[0], partner_weight, partner_moment, x_rows)
    widths = [width for _, width in chunks(BWD_PARTS, features)]
    count = len(widths)
    cots = list(norm_cot(residual_in, upstream, norm_gain, keeps, gots, widths))

    half = rows // 2
    nbs = [from_mate(cot, 2) for cot in cots]
    mates = [from_mate(cot, 1) for cot in cots]
    kept, got, ours, theirs = [], [], [], []

    def gather(i):
        both = kept[i] + got[i].astype(F32)
        total = both[:half]
        for d in range(1, n_quad):
            total += shift_far(both[d * half : (d + 1) * half].astype(BF), d).astype(F32)
        ours.append(total)
        theirs.append(from_partner(total.astype(BF)))

    far_sums = []

    def sum_far(i):
        both = kept[i] + got[i].astype(F32)
        far_sums.append(
            [shift_far(both[d * half : (d + 1) * half].astype(BF), d) for d in range(1, n_quad)]
        )
        ours.append(both[:half])

    def give_back(i):
        for block in far_sums[i]:
            ours[i] += block.astype(F32)
        theirs.append(from_partner(ours[i].astype(BF)))

    nb_mates = [from_mate(nb, 1) for nb in nbs]
    for i in range(count + 2):
        if i < count:
            seen = got[-1:] + (far_sums[-1] if far_sums else []) + theirs[-1:]
            if i == count - 1:
                ig_own, ig_nb = input_grad_part(
                    place, own, mate, [after(cots[0], kept[-1])] + cots[1:], nbs, pieces, scale
                )
                seen += [ig_nb]
            keep, give = gradient_part(
                after(x_rows, *seen) if seen else x_rows, [cots[i], nbs[i], mates[i], nb_mates[i]], scale
            )
            kept.append(keep)
        if 0 <= i - 2:
            give_back(i - 2)
        if 0 <= i - 1 < count:
            sum_far(i - 1)
        if i < count:
            got.append(from_partner(give))

    ig_got = from_mate(ig_nb, 2)
    input_grad = interleave(near.reshape(1).astype(jnp.int32), ig_own, ig_got, n_quad)

    new_weight, new_momentum = update(
        side.reshape(1).astype(jnp.int32), weight, partner_weight, momentum, partner_moment, ours, theirs
    )
    return (input_grad, new_weight, new_momentum)


def solution(mesh):
    return jax.shard_map(
        per_device,
        mesh=mesh,
        in_specs=(
            P(("rep", "fsdp"), None),
            P(("rep", "fsdp"), None),
            P(("rep", "fsdp"), None),
            P(),
            P("rep", "fsdp", None),
            P("rep", "fsdp", None),
        ),
        out_specs=(P(("rep", "fsdp"), None), P("rep", "fsdp", None), P("rep", "fsdp", None)),
        check_vma=False,
    )
```

```python
import functools
import math

import jax
import jax.numpy as jnp
from jax import lax
from jax.experimental import pallas as pl
from jax.experimental.pallas import tpu as pltpu
from jax.sharding import PartitionSpec as P

PARTNER_BIT = 1

EPSILON = 1e-05
LEARN_RATE = 0.05
MOMENTUM_DECAY = 0.9

FWD_PARTS = (8, 8, 4)
BWD_PARTS = (8, 8, 4)
SWAP_PARTS = 2
GIVE_PARTS = 1
COST_SHARE = 0.01
VMEM_MIB = 48
BF = jnp.bfloat16
F32 = jnp.float32


def params(mib=VMEM_MIB):
    return pltpu.CompilerParams(vmem_limit_bytes=mib << 20)


def cost(flops, moved):
    return pl.CostEstimate(
        flops=int(flops * COST_SHARE), bytes_accessed=int(moved * COST_SHARE), transcendentals=0
    )


def whole(*shape):
    return pl.BlockSpec(shape, lambda *_: (0,) * len(shape))


def after(block, *others):
    return lax.optimization_barrier((block, *others))[0]


def from_partner(block):
    count = lax.axis_size("rep")
    return lax.ppermute(block, "rep", [(g, g ^ (1 << PARTNER_BIT)) for g in range(count)])


def from_mate(block, bit):
    count = lax.axis_size("fsdp")
    return lax.ppermute(block, "fsdp", [(f, f ^ bit) for f in range(count)])


def shift_far(block, hops):
    count = lax.axis_size("fsdp")
    return lax.ppermute(block, "fsdp", [(f, (f + 4 * hops) % count) for f in range(count)])


def chunks(parts, features):
    unit = features // sum(parts)
    return [(sum(parts[:i]) * unit, part * unit) for i, part in enumerate(parts)]


def put_rows(place, rows, refs, w_ref, start):
    block = done = 0
    for ref in refs:
        count = ref.shape[0]
        at = pl.ds(pl.multiple_of(place[block] * rows + done, 8), count)
        w_ref[at, start : start + ref.shape[1]] = ref[...]
        done += count
        if done == rows:
            block, done = block + 1, 0


def forward_kernel(scale, rows, parts, place, x_ref, nb_ref, *refs):
    pieces, w_ref = refs[: -2 * parts - 1], refs[-1]
    keeps, gives = refs[-2 * parts - 1 : -parts - 1], refs[-parts - 1 : -1]
    put_rows(place, rows, pieces, w_ref, 0)
    x = jnp.concatenate([x_ref[...], nb_ref[...]], axis=0)
    part = jnp.dot(x, w_ref[...], preferred_element_type=F32) * scale
    tokens, width = keeps[0].shape
    for i in range(parts):
        cols = slice(i * width, (i + 1) * width)
        keeps[i][...] = part[:tokens, cols]
        gives[i][...] = part[tokens:, cols].astype(BF)


def forward_part(place, x_own, x_nb, weights, scale, parts):
    tokens, depth = x_own.shape
    rows, width = weights[0].shape
    operands = (x_own, x_nb, *weights)
    out = pl.pallas_call(
        functools.partial(forward_kernel, scale, rows, parts),
        grid_spec=pltpu.PrefetchScalarGridSpec(
            num_scalar_prefetch=1,
            grid=(1,),
            in_specs=[whole(*a.shape) for a in operands],
            out_specs=[whole(tokens, width // parts)] * (2 * parts),
            scratch_shapes=[pltpu.VMEM((depth, width), BF)],
        ),
        out_shape=[
            jax.ShapeDtypeStruct((tokens, width // parts), kind)
            for kind in (F32, BF)
            for _ in range(parts)
        ],
        compiler_params=params(),
        cost_estimate=cost(4 * tokens * depth * width, 2 * depth * (2 * width + 2 * tokens)),
        name="forward_part",
    )(place, *operands)
    return out[:parts], out[parts:]


def norm_kernel(n_in, n_out, res_ref, up_ref, gain_ref, *refs):
    keeps, gots, cots = refs[:n_in], refs[n_in : 2 * n_in], refs[2 * n_in :]
    features = res_ref.shape[1]
    summed, scaled = [], []
    square = inner = 0.0
    start = 0
    for keep, got in zip(keeps, gots):
        cols = slice(start, start + keep.shape[1])
        start = cols.stop
        s = res_ref[:, cols].astype(F32) + (keep[...] + got[...].astype(F32))
        c = up_ref[:, cols].astype(F32) * gain_ref[:, cols]
        square += jnp.sum(s * s, axis=-1, keepdims=True)
        inner += jnp.sum(c * s, axis=-1, keepdims=True)
        summed.append(s)
        scaled.append(c)
    inv_rms = lax.rsqrt(square / features + EPSILON)
    pull = inner / features * inv_rms * inv_rms
    start = 0
    for s, c in zip(summed, scaled):
        cot = (inv_rms * (c - s * pull)).astype(BF)
        end = start + s.shape[1]
        first = 0
        for ref in cots:
            last = first + ref.shape[1]
            low, high = max(first, start), min(last, end)
            if low < high:
                ref[:, low - first : high - first] = cot[:, low - start : high - start]
            first = last
        start = end


def norm_cot(residual, upstream, gain, keeps, gots, widths):
    tokens, features = residual.shape
    tile = 64
    row = lambda w: pl.BlockSpec((tile, w), lambda i: (i, 0))
    return pl.pallas_call(
        functools.partial(norm_kernel, len(keeps), len(widths)),
        grid=(tokens // tile,),
        in_specs=[row(features), row(features), pl.BlockSpec((1, features), lambda i: (0, 0))]
        + [row(keep.shape[1]) for keep in keeps] * 2,
        out_specs=[row(w) for w in widths],
        out_shape=[jax.ShapeDtypeStruct((tokens, w), BF) for w in widths],
        compiler_params=params(),
        cost_estimate=cost(20 * tokens * features, 12 * tokens * features),
        name="norm_cot",
    )(residual, upstream, gain.reshape(1, features), *keeps, *gots)


def turn_kernel(rows, place, x_ref, nb_ref, mine_ref, theirs_ref, turned_ref):
    tokens = x_ref.shape[0]
    turned_ref[:, :tokens] = x_ref[...].astype(F32).T
    turned_ref[:, tokens:] = nb_ref[...].astype(F32).T
    half = rows // 2
    n_quad = mine_ref.shape[0] // rows
    for to in range(2):
        for d in range(n_quad):
            low = (to * n_quad + d) * half
            for ref, core in ((mine_ref, 0), (theirs_ref, 1)):
                at = place[2 * d + core] * rows + (place[2 * n_quad] ^ to) * half
                block = turned_ref[pl.ds(pl.multiple_of(at, 8), half), :]
                ref[low : low + half, :] = block.astype(BF)


def turn(place, x_own, x_nb, rows):
    tokens, depth = x_own.shape
    full = lambda shape: pl.BlockSpec(shape, lambda i, place: (0, 0))
    return pl.pallas_call(
        functools.partial(turn_kernel, rows),
        grid_spec=pltpu.PrefetchScalarGridSpec(
            num_scalar_prefetch=1,
            grid=(1,),
            in_specs=[full(x_own.shape)] * 2,
            out_specs=[full((depth // 2, 2 * tokens))] * 2,
            scratch_shapes=[pltpu.VMEM((depth, 2 * tokens), F32)],
        ),
        out_shape=[jax.ShapeDtypeStruct((depth // 2, 2 * tokens), BF)] * 2,
        compiler_params=params(),
        cost_estimate=cost(0, 8 * depth * tokens),
        name="turn",
    )(place, x_own, x_nb)


def gradient_kernel(scale, x_ref, *refs):
    cots, (keep_ref, give_ref) = refs[:4], refs[4:]
    cot = jnp.concatenate([ref[...] for ref in cots], axis=0)
    part = jnp.dot(x_ref[...], cot, preferred_element_type=F32) * scale
    half = keep_ref.shape[0]
    keep_ref[...] = part[:half]
    give_ref[...] = part[half:].astype(BF)


def gradient_part(x_rows, cots, scale):
    rows, tokens = x_rows.shape
    width = cots[0].shape[1]
    return pl.pallas_call(
        functools.partial(gradient_kernel, scale),
        grid=(1,),
        in_specs=[whole(*a.shape) for a in (x_rows, *cots)],
        out_specs=[whole(rows // 2, width)] * 2,
        out_shape=[
            jax.ShapeDtypeStruct((rows // 2, width), F32),
            jax.ShapeDtypeStruct((rows // 2, width), BF),
        ],
        compiler_params=params(),
        cost_estimate=cost(2 * rows * tokens * width, 2 * tokens * (rows + width) + 3 * rows * width),
        name="gradient_part",
    )(x_rows, *cots)


def input_grad_kernel(scale, rows, n_cot, counts, place, *refs):
    cots, weights, (out_ref, w_ref) = refs[:n_cot], refs[n_cot:-2], refs[-2:]
    start = first = 0
    for count in counts:
        part = weights[first : first + count]
        put_rows(place, rows, part, w_ref, start)
        first += count
        start += part[0].shape[1]
    cot = jnp.concatenate([ref[...] for ref in cots], axis=1)
    total = lax.dot_general(cot, w_ref[...], (((1,), (1,)), ((), ())), preferred_element_type=F32)
    out_ref[...] = (total * scale).astype(BF)


def input_grad_part(place, cots, weights, scale):
    tokens = cots[0].shape[0]
    features = sum(cot.shape[1] for cot in cots)
    rows = weights[0][0].shape[0]
    depth = sum(w.shape[0] for w in weights[0])
    operands = [*cots] + [w for chunk in weights for w in chunk]
    return pl.pallas_call(
        functools.partial(input_grad_kernel, scale, rows, len(cots), [len(w) for w in weights]),
        grid_spec=pltpu.PrefetchScalarGridSpec(
            num_scalar_prefetch=1,
            grid=(1,),
            in_specs=[whole(*a.shape) for a in operands],
            out_specs=whole(tokens, depth),
            scratch_shapes=[pltpu.VMEM((depth, features), BF)],
        ),
        out_shape=jax.ShapeDtypeStruct((tokens, depth), BF),
        compiler_params=params(),
        cost_estimate=cost(
            2 * tokens * depth * features, 2 * depth * features + 2 * tokens * (depth + features)
        ),
        name="input_grad_part",
    )(place, *operands)


def split_kernel(n_quad, near, mixed_ref, own_ref, give_ref):
    width = own_ref.shape[1] // n_quad
    for side in range(2):

        @pl.when(near[0] == side)
        def _():
            for i in range(n_quad):
                to = slice(i * width, (i + 1) * width)
                ours, theirs = 2 * i + side, 2 * i + 1 - side
                own_ref[:, to] = mixed_ref[:, ours * width : (ours + 1) * width]
                give_ref[:, to] = mixed_ref[:, theirs * width : (theirs + 1) * width]


def split(near, mixed, n_quad):
    tokens, features = mixed.shape
    tile = 64
    row = lambda w: pl.BlockSpec((tile, w), lambda i, near: (i, 0))
    return pl.pallas_call(
        functools.partial(split_kernel, n_quad),
        grid_spec=pltpu.PrefetchScalarGridSpec(
            num_scalar_prefetch=1,
            grid=(tokens // tile,),
            in_specs=[row(features)],
            out_specs=[row(features // 2)] * 2,
        ),
        out_shape=[jax.ShapeDtypeStruct((tokens, features // 2), BF)] * 2,
        compiler_params=params(),
        cost_estimate=cost(0, 4 * tokens * features),
        name="split",
    )(near, mixed)


def interleave_kernel(n_quad, near, own_ref, got_ref, out_ref):
    width = own_ref.shape[1] // n_quad
    for side in range(2):

        @pl.when(near[0] == side)
        def _():
            for i in range(n_quad):
                at = slice(i * width, (i + 1) * width)
                ours, theirs = 2 * i + side, 2 * i + 1 - side
                out_ref[:, ours * width : (ours + 1) * width] = own_ref[:, at]
                out_ref[:, theirs * width : (theirs + 1) * width] = got_ref[:, at]


def interleave(near, own, got, n_quad):
    tokens, depth = own.shape
    tile = 64
    row = lambda w: pl.BlockSpec((tile, w), lambda i, near: (i, 0))
    return pl.pallas_call(
        functools.partial(interleave_kernel, n_quad),
        grid_spec=pltpu.PrefetchScalarGridSpec(
            num_scalar_prefetch=1,
            grid=(tokens // tile,),
            in_specs=[row(depth)] * 2,
            out_specs=row(2 * depth),
        ),
        out_shape=jax.ShapeDtypeStruct((tokens, 2 * depth), BF),
        compiler_params=params(),
        cost_estimate=cost(0, 8 * tokens * depth),
        name="interleave",
    )(near, own, got)


def update_kernel(w_ref, pw_ref, m_ref, pm_ref, ours_ref, theirs_ref, *refs):
    weight_ref, moment_ref = refs[-2:]
    mine = pl.program_id(0) == 0
    grads = jnp.where(mine, ours_ref[...], theirs_ref[...].astype(F32))
    moment = 0.5 * (MOMENTUM_DECAY * (m_ref[0] + pm_ref[...].astype(F32)) + grads)
    moment_ref[0] = moment
    both = w_ref[0].astype(F32) + pw_ref[...].astype(F32)
    weight_ref[0] = (0.5 * both - LEARN_RATE * moment).astype(BF)


def update(side, weight, partner_weight, momentum, partner_moment, ours, theirs, start, made):
    _, rows, _ = weight.shape
    half, width = ours.shape
    unit = math.gcd(start, width)
    at = start // unit
    block3 = pl.BlockSpec((1, half, unit), lambda i, j, side: (0, (side[0] + i) % 2, at + j))
    block2 = pl.BlockSpec((half, unit), lambda i, j, side: ((side[0] + i) % 2, at + j))
    fixed = pl.BlockSpec((half, unit), lambda i, j, side: (0, j))

    def kernel(side, *refs):
        update_kernel(*refs)

    return pl.pallas_call(
        kernel,
        grid_spec=pltpu.PrefetchScalarGridSpec(
            num_scalar_prefetch=1,
            grid=(2, width // unit),
            in_specs=[block3, block2, block3, block2, fixed, fixed]
            + [pl.BlockSpec(memory_space=pl.ANY)] * len(made),
            out_specs=[block3, block3],
        ),
        out_shape=[
            jax.ShapeDtypeStruct(weight.shape, BF),
            jax.ShapeDtypeStruct(momentum.shape, F32),
        ],
        input_output_aliases={7 + i: i for i in range(len(made))},
        compiler_params=params(),
        cost_estimate=cost(10 * rows * width, 18 * rows * width),
        name="update",
    )(side, weight, partner_weight, momentum, partner_moment, ours, theirs, *made)


def per_device(residual_in, mixed, upstream, norm_gain, weight, momentum):
    tokens, features = mixed.shape
    scale = features ** (-0.5)
    count = lax.axis_size("fsdp")
    n_quad = count // 4
    rows = weight.shape[1]
    me = lax.axis_index("fsdp")
    quad, core, near = me // 4, me % 2, (me // 2) % 2
    side = (lax.axis_index("rep") >> PARTNER_BIT) & 1
    own = weight[0]

    cols = chunks(FWD_PARTS, features)
    slices = [own[:, start : start + width] for start, width in cols]
    x_own, x_give = split(near.reshape(1).astype(jnp.int32), after(mixed, *slices), n_quad)
    x_nb = from_mate(x_give, 2)
    small_moment = momentum[0].astype(BF)
    mates = [from_mate(piece, 1) for piece in slices]
    partner_weight = from_partner(own)
    partner_moment = from_partner(small_moment)

    quads = [quad] + [(quad + n_quad - d) % n_quad for d in range(1, n_quad)]
    place = jnp.stack(
        [quads[0] * 2 + core, quads[0] * 2 + 1 - core]
        + [q * 2 + core for q in quads[1:]]
        + [q * 2 + 1 - core for q in quads[1:]]
    ).astype(jnp.int32)

    on = [(quad + d) % n_quad for d in range(n_quad)]
    order = jnp.stack([2 * q + c for q in on for c in (core, 1 - core)] + [side]).astype(jnp.int32)

    def send_far(i, *others):
        piece = after(slices[i], *fars[-1], *others) if i else slices[i]
        fars.append([shift_far(piece, d) for d in range(1, n_quad)])

    def swap_rows(block, parts):
        parts = parts if rows % (16 * parts) == 0 else 1
        return [from_mate(part, 1) for part in jnp.split(block, parts, axis=0)]

    fars, pieces, keeps, gots = [], [], [], []
    send_far(0)
    send_far(1)
    last = len(cols) - 1
    for i in range(len(cols)):
        seen = keeps[-1:]
        if i == last:
            x_mine, x_theirs = turn(order, after(x_own, keeps[-1]), x_nb, rows)
            x_rows = jnp.concatenate([x_mine, from_mate(x_theirs, 1)], axis=1)
        if i == last:
            seen += gots[:1] + [partner_weight]
        parts = SWAP_PARTS if i == last else 1
        far_mates = [p for w in fars[i] for p in swap_rows(after(w, *seen) if seen else w, parts)]
        pieces.append([slices[i], mates[i]] + fars[i] + far_mates)
        kept, given = forward_part(place, x_own, x_nb, pieces[i], scale, GIVE_PARTS)
        keeps += kept
        gots += [from_mate(give, 2) for give in given]
        if i + 2 <= last:
            send_far(i + 2)

    keeps[0] = after(keeps[0], partner_moment, x_rows)
    widths = [width for _, width in chunks(BWD_PARTS, features)]
    count = len(widths)
    cots = list(norm_cot(residual_in, upstream, norm_gain, keeps, gots, widths))

    half = rows // 2
    nbs = [from_mate(cot, 2) for cot in cots]
    mates = [from_mate(cot, 1) for cot in cots]
    kept, got, ours, theirs = [], [], [], []

    def gather(i):
        both = kept[i] + got[i].astype(F32)
        total = both[:half]
        for d in range(1, n_quad):
            total += shift_far(both[d * half : (d + 1) * half].astype(BF), d).astype(F32)
        ours.append(total)
        theirs.append(from_partner(total.astype(BF)))

    far_sums = []

    def sum_far(i):
        both = kept[i] + got[i].astype(F32)
        far_sums.append(
            [shift_far(both[d * half : (d + 1) * half].astype(BF), d) for d in range(1, n_quad)]
        )
        ours.append(both[:half])

    made, first_made, ig_own = [], [], []

    def give_back(i):
        total = ours[i]
        for block in far_sums[i]:
            total += block.astype(F32)
        if i == 1:
            total = after(total, ig_own[0])
        if i == count - 1:
            total = after(total, first_made[0])
        ours[i] = total
        theirs.append(from_partner(total.astype(BF)))

    def finish(i):
        start = chunks(BWD_PARTS, features)[i][0]
        made[:] = update(
            side.reshape(1).astype(jnp.int32),
            weight,
            partner_weight,
            momentum,
            partner_moment,
            ours[i],
            theirs[i],
            start,
            made,
        )
        first_made.append(made[0])

    nb_mates = [from_mate(nb, 1) for nb in nbs]
    for i in range(count + 2):
        if i < count:
            seen = kept[-1:]
            if i == 1:
                seen += nb_mates[2:]
            if i == 2:
                seen += [ig_nb]
            x_seen = after(x_rows, *seen) if seen else x_rows
            keep, give = gradient_part(x_seen, [cots[i], nbs[i], mates[i], nb_mates[i]], scale)
            kept.append(keep)
            got.append(from_partner(after(give, *got[-1:]) if got else give))
            if i == 1:
                first_nb = after(nbs[0], keep)
                ig_nb = input_grad_part(place, [first_nb] + nbs[1:], pieces, scale)
                ig_got = from_mate(ig_nb, 2)
            if i == 2:
                first_cot = after(cots[0], kept[-1])
                ig_own.append(input_grad_part(place, [first_cot] + cots[1:], pieces, scale))
        if 0 <= i - 2:
            give_back(i - 2)
            if i - 2 < count - 1:
                finish(i - 2)
        if 0 <= i - 1 < count:
            sum_far(i - 1)

    input_grad = interleave(near.reshape(1).astype(jnp.int32), ig_own[0], ig_got, n_quad)

    finish(count - 1)
    new_weight, new_momentum = made
    return (input_grad, new_weight, new_momentum)


def solution(mesh):
    return jax.shard_map(
        per_device,
        mesh=mesh,
        in_specs=(
            P(("rep", "fsdp"), None),
            P(("rep", "fsdp"), None),
            P(("rep", "fsdp"), None),
            P(),
            P("rep", "fsdp", None),
            P("rep", "fsdp", None),
        ),
        out_specs=(P(("rep", "fsdp"), None), P("rep", "fsdp", None), P("rep", "fsdp", None)),
        check_vma=False,
    )
```

```python
import functools
import math

import jax
import jax.numpy as jnp
from jax import lax
from jax.experimental import pallas as pl
from jax.experimental.pallas import tpu as pltpu
from jax.sharding import PartitionSpec as P

PARTNER_BIT = 1

EPSILON = 1e-05
LEARN_RATE = 0.05
MOMENTUM_DECAY = 0.9

FWD_PARTS = (8, 8, 4)
BWD_PARTS = (8, 8, 4)
SWAP_PARTS = 2
GIVE_PARTS = 1
COST_SHARE = 0.01
VMEM_MIB = 36
BF = jnp.bfloat16
F32 = jnp.float32


def params(mib=VMEM_MIB):
    return pltpu.CompilerParams(vmem_limit_bytes=mib << 20)


def cost(flops, moved):
    return pl.CostEstimate(
        flops=int(flops * COST_SHARE), bytes_accessed=int(moved * COST_SHARE), transcendentals=0
    )


def whole(*shape):
    return pl.BlockSpec(shape, lambda *_: (0,) * len(shape))


def after(block, *others):
    return lax.optimization_barrier((block, *others))[0]


def from_partner(block):
    count = lax.axis_size("rep")
    return lax.ppermute(block, "rep", [(g, g ^ (1 << PARTNER_BIT)) for g in range(count)])


def from_mate(block, bit):
    count = lax.axis_size("fsdp")
    return lax.ppermute(block, "fsdp", [(f, f ^ bit) for f in range(count)])


def shift_far(block, hops):
    count = lax.axis_size("fsdp")
    return lax.ppermute(block, "fsdp", [(f, (f + 4 * hops) % count) for f in range(count)])


def chunks(parts, features):
    unit = features // sum(parts)
    return [(sum(parts[:i]) * unit, part * unit) for i, part in enumerate(parts)]


def put_rows(place, rows, refs, w_ref, start):
    block = done = 0
    for ref in refs:
        count = ref.shape[0]
        at = pl.ds(pl.multiple_of(place[block] * rows + done, 8), count)
        w_ref[at, start : start + ref.shape[1]] = ref[...]
        done += count
        if done == rows:
            block, done = block + 1, 0


def forward_kernel(scale, rows, parts, place, x_ref, nb_ref, *refs):
    pieces, w_ref = refs[: -2 * parts - 1], refs[-1]
    keeps, gives = refs[-2 * parts - 1 : -parts - 1], refs[-parts - 1 : -1]
    put_rows(place, rows, pieces, w_ref, 0)
    x = jnp.concatenate([x_ref[...], nb_ref[...]], axis=0)
    part = jnp.dot(x, w_ref[...], preferred_element_type=F32) * scale
    tokens, width = keeps[0].shape
    for i in range(parts):
        cols = slice(i * width, (i + 1) * width)
        keeps[i][...] = part[:tokens, cols]
        gives[i][...] = part[tokens:, cols].astype(BF)


def forward_part(place, x_own, x_nb, weights, scale, parts):
    tokens, depth = x_own.shape
    rows, width = weights[0].shape
    operands = (x_own, x_nb, *weights)
    out = pl.pallas_call(
        functools.partial(forward_kernel, scale, rows, parts),
        grid_spec=pltpu.PrefetchScalarGridSpec(
            num_scalar_prefetch=1,
            grid=(1,),
            in_specs=[whole(*a.shape) for a in operands],
            out_specs=[whole(tokens, width // parts)] * (2 * parts),
            scratch_shapes=[pltpu.VMEM((depth, width), BF)],
        ),
        out_shape=[
            jax.ShapeDtypeStruct((tokens, width // parts), kind)
            for kind in (F32, BF)
            for _ in range(parts)
        ],
        compiler_params=params(),
        cost_estimate=cost(4 * tokens * depth * width, 2 * depth * (2 * width + 2 * tokens)),
        name="forward_part",
    )(place, *operands)
    return out[:parts], out[parts:]


def norm_kernel(n_in, n_out, res_ref, up_ref, gain_ref, *refs):
    keeps, gots, cots = refs[:n_in], refs[n_in : 2 * n_in], refs[2 * n_in :]
    features = res_ref.shape[1]
    summed, scaled = [], []
    square = inner = 0.0
    start = 0
    for keep, got in zip(keeps, gots):
        cols = slice(start, start + keep.shape[1])
        start = cols.stop
        s = res_ref[:, cols].astype(F32) + (keep[...] + got[...].astype(F32))
        c = up_ref[:, cols].astype(F32) * gain_ref[:, cols]
        square += jnp.sum(s * s, axis=-1, keepdims=True)
        inner += jnp.sum(c * s, axis=-1, keepdims=True)
        summed.append(s)
        scaled.append(c)
    inv_rms = lax.rsqrt(square / features + EPSILON)
    pull = inner / features * inv_rms * inv_rms
    start = 0
    for s, c in zip(summed, scaled):
        cot = (inv_rms * (c - s * pull)).astype(BF)
        end = start + s.shape[1]
        first = 0
        for ref in cots:
            last = first + ref.shape[1]
            low, high = max(first, start), min(last, end)
            if low < high:
                ref[:, low - first : high - first] = cot[:, low - start : high - start]
            first = last
        start = end


def norm_cot(residual, upstream, gain, keeps, gots, widths):
    tokens, features = residual.shape
    tile = 64
    row = lambda w: pl.BlockSpec((tile, w), lambda i: (i, 0))
    return pl.pallas_call(
        functools.partial(norm_kernel, len(keeps), len(widths)),
        grid=(tokens // tile,),
        in_specs=[row(features), row(features), pl.BlockSpec((1, features), lambda i: (0, 0))]
        + [row(keep.shape[1]) for keep in keeps] * 2,
        out_specs=[row(w) for w in widths],
        out_shape=[jax.ShapeDtypeStruct((tokens, w), BF) for w in widths],
        compiler_params=params(),
        cost_estimate=cost(20 * tokens * features, 12 * tokens * features),
        name="norm_cot",
    )(residual, upstream, gain.reshape(1, features), *keeps, *gots)


def turn_kernel(rows, place, x_ref, nb_ref, mine_ref, theirs_ref, turned_ref):
    tokens = x_ref.shape[0]
    turned_ref[:, :tokens] = x_ref[...].astype(F32).T
    turned_ref[:, tokens:] = nb_ref[...].astype(F32).T
    half = rows // 2
    n_quad = mine_ref.shape[0] // rows
    for to in range(2):
        for d in range(n_quad):
            low = (to * n_quad + d) * half
            for ref, core in ((mine_ref, 0), (theirs_ref, 1)):
                at = place[2 * d + core] * rows + (place[2 * n_quad] ^ to) * half
                block = turned_ref[pl.ds(pl.multiple_of(at, 8), half), :]
                ref[low : low + half, :] = block.astype(BF)


def turn(place, x_own, x_nb, rows):
    tokens, depth = x_own.shape
    full = lambda shape: pl.BlockSpec(shape, lambda i, place: (0, 0))
    return pl.pallas_call(
        functools.partial(turn_kernel, rows),
        grid_spec=pltpu.PrefetchScalarGridSpec(
            num_scalar_prefetch=1,
            grid=(1,),
            in_specs=[full(x_own.shape)] * 2,
            out_specs=[full((depth // 2, 2 * tokens))] * 2,
            scratch_shapes=[pltpu.VMEM((depth, 2 * tokens), F32)],
        ),
        out_shape=[jax.ShapeDtypeStruct((depth // 2, 2 * tokens), BF)] * 2,
        compiler_params=params(),
        cost_estimate=cost(0, 8 * depth * tokens),
        name="turn",
    )(place, x_own, x_nb)


def gradient_kernel(scale, x_ref, *refs):
    cots, (keep_ref, give_ref) = refs[:4], refs[4:]
    cot = jnp.concatenate([ref[...] for ref in cots], axis=0)
    part = jnp.dot(x_ref[...], cot, preferred_element_type=F32) * scale
    half = keep_ref.shape[0]
    keep_ref[...] = part[:half]
    give_ref[...] = part[half:].astype(BF)


def gradient_part(x_rows, cots, scale):
    rows, tokens = x_rows.shape
    width = cots[0].shape[1]
    return pl.pallas_call(
        functools.partial(gradient_kernel, scale),
        grid=(1,),
        in_specs=[whole(*a.shape) for a in (x_rows, *cots)],
        out_specs=[whole(rows // 2, width)] * 2,
        out_shape=[
            jax.ShapeDtypeStruct((rows // 2, width), F32),
            jax.ShapeDtypeStruct((rows // 2, width), BF),
        ],
        compiler_params=params(),
        cost_estimate=cost(2 * rows * tokens * width, 2 * tokens * (rows + width) + 3 * rows * width),
        name="gradient_part",
    )(x_rows, *cots)


def input_grad_kernel(scale, rows, n_cot, counts, place, *refs):
    cots, weights, (out_ref, w_ref) = refs[:n_cot], refs[n_cot:-2], refs[-2:]
    start = first = 0
    for count in counts:
        part = weights[first : first + count]
        put_rows(place, rows, part, w_ref, start)
        first += count
        start += part[0].shape[1]
    cot = jnp.concatenate([ref[...] for ref in cots], axis=1)
    total = lax.dot_general(cot, w_ref[...], (((1,), (1,)), ((), ())), preferred_element_type=F32)
    out_ref[...] = (total * scale).astype(BF)


def input_grad_part(place, cots, weights, scale):
    tokens = cots[0].shape[0]
    features = sum(cot.shape[1] for cot in cots)
    rows = weights[0][0].shape[0]
    depth = sum(w.shape[0] for w in weights[0])
    operands = [*cots] + [w for chunk in weights for w in chunk]
    return pl.pallas_call(
        functools.partial(input_grad_kernel, scale, rows, len(cots), [len(w) for w in weights]),
        grid_spec=pltpu.PrefetchScalarGridSpec(
            num_scalar_prefetch=1,
            grid=(1,),
            in_specs=[whole(*a.shape) for a in operands],
            out_specs=whole(tokens, depth),
            scratch_shapes=[pltpu.VMEM((depth, features), BF)],
        ),
        out_shape=jax.ShapeDtypeStruct((tokens, depth), BF),
        compiler_params=params(),
        cost_estimate=cost(
            2 * tokens * depth * features, 2 * depth * features + 2 * tokens * (depth + features)
        ),
        name="input_grad_part",
    )(place, *operands)


def split_kernel(n_quad, near, mixed_ref, own_ref, give_ref):
    width = own_ref.shape[1] // n_quad
    for side in range(2):

        @pl.when(near[0] == side)
        def _():
            for i in range(n_quad):
                to = slice(i * width, (i + 1) * width)
                ours, theirs = 2 * i + side, 2 * i + 1 - side
                own_ref[:, to] = mixed_ref[:, ours * width : (ours + 1) * width]
                give_ref[:, to] = mixed_ref[:, theirs * width : (theirs + 1) * width]


def split(near, mixed, n_quad):
    tokens, features = mixed.shape
    tile = 64
    row = lambda w: pl.BlockSpec((tile, w), lambda i, near: (i, 0))
    return pl.pallas_call(
        functools.partial(split_kernel, n_quad),
        grid_spec=pltpu.PrefetchScalarGridSpec(
            num_scalar_prefetch=1,
            grid=(tokens // tile,),
            in_specs=[row(features)],
            out_specs=[row(features // 2)] * 2,
        ),
        out_shape=[jax.ShapeDtypeStruct((tokens, features // 2), BF)] * 2,
        compiler_params=params(),
        cost_estimate=cost(0, 4 * tokens * features),
        name="split",
    )(near, mixed)


def interleave_kernel(n_quad, near, own_ref, got_ref, out_ref):
    width = own_ref.shape[1] // n_quad
    for side in range(2):

        @pl.when(near[0] == side)
        def _():
            for i in range(n_quad):
                at = slice(i * width, (i + 1) * width)
                ours, theirs = 2 * i + side, 2 * i + 1 - side
                out_ref[:, ours * width : (ours + 1) * width] = own_ref[:, at]
                out_ref[:, theirs * width : (theirs + 1) * width] = got_ref[:, at]


def interleave(near, own, got, n_quad):
    tokens, depth = own.shape
    tile = 64
    row = lambda w: pl.BlockSpec((tile, w), lambda i, near: (i, 0))
    return pl.pallas_call(
        functools.partial(interleave_kernel, n_quad),
        grid_spec=pltpu.PrefetchScalarGridSpec(
            num_scalar_prefetch=1,
            grid=(tokens // tile,),
            in_specs=[row(depth)] * 2,
            out_specs=row(2 * depth),
        ),
        out_shape=jax.ShapeDtypeStruct((tokens, 2 * depth), BF),
        compiler_params=params(),
        cost_estimate=cost(0, 8 * tokens * depth),
        name="interleave",
    )(near, own, got)


def update_kernel(w_ref, pw_ref, m_ref, pm_ref, ours_ref, theirs_ref, *refs):
    weight_ref, moment_ref = refs[-2:]
    mine = pl.program_id(0) == 0
    grads = jnp.where(mine, ours_ref[...], theirs_ref[...].astype(F32))
    moment = 0.5 * (MOMENTUM_DECAY * (m_ref[0] + pm_ref[...].astype(F32)) + grads)
    moment_ref[0] = moment
    both = w_ref[0].astype(F32) + pw_ref[...].astype(F32)
    weight_ref[0] = (0.5 * both - LEARN_RATE * moment).astype(BF)


def update(side, weight, partner_weight, momentum, partner_moment, ours, theirs, start, made):
    _, rows, _ = weight.shape
    half, width = ours.shape
    unit = math.gcd(start, width)
    at = start // unit
    block3 = pl.BlockSpec((1, half, unit), lambda i, j, side: (0, (side[0] + i) % 2, at + j))
    block2 = pl.BlockSpec((half, unit), lambda i, j, side: ((side[0] + i) % 2, at + j))
    fixed = pl.BlockSpec((half, unit), lambda i, j, side: (0, j))

    def kernel(side, *refs):
        update_kernel(*refs)

    return pl.pallas_call(
        kernel,
        grid_spec=pltpu.PrefetchScalarGridSpec(
            num_scalar_prefetch=1,
            grid=(2, width // unit),
            in_specs=[block3, block2, block3, block2, fixed, fixed]
            + [pl.BlockSpec(memory_space=pl.ANY)] * len(made),
            out_specs=[block3, block3],
        ),
        out_shape=[
            jax.ShapeDtypeStruct(weight.shape, BF),
            jax.ShapeDtypeStruct(momentum.shape, F32),
        ],
        input_output_aliases={7 + i: i for i in range(len(made))},
        compiler_params=params(),
        cost_estimate=cost(10 * rows * width, 18 * rows * width),
        name="update",
    )(side, weight, partner_weight, momentum, partner_moment, ours, theirs, *made)


def per_device(residual_in, mixed, upstream, norm_gain, weight, momentum):
    tokens, features = mixed.shape
    scale = features ** (-0.5)
    count = lax.axis_size("fsdp")
    n_quad = count // 4
    rows = weight.shape[1]
    me = lax.axis_index("fsdp")
    quad, core, near = me // 4, me % 2, (me // 2) % 2
    side = (lax.axis_index("rep") >> PARTNER_BIT) & 1
    own = weight[0]

    cols = chunks(FWD_PARTS, features)
    slices = [own[:, start : start + width] for start, width in cols]
    x_own, x_give = split(near.reshape(1).astype(jnp.int32), after(mixed, *slices), n_quad)
    x_nb = from_mate(x_give, 2)
    small_moment = momentum[0].astype(BF)
    mates = [from_mate(piece, 1) for piece in slices]
    partner_weight = from_partner(own)
    partner_moment = from_partner(small_moment)

    quads = [quad] + [(quad + n_quad - d) % n_quad for d in range(1, n_quad)]
    place = jnp.stack(
        [quads[0] * 2 + core, quads[0] * 2 + 1 - core]
        + [q * 2 + core for q in quads[1:]]
        + [q * 2 + 1 - core for q in quads[1:]]
    ).astype(jnp.int32)

    on = [(quad + d) % n_quad for d in range(n_quad)]
    order = jnp.stack([2 * q + c for q in on for c in (core, 1 - core)] + [side]).astype(jnp.int32)

    def send_far(i, *others):
        piece = after(slices[i], *fars[-1], *others) if i else slices[i]
        fars.append([shift_far(piece, d) for d in range(1, n_quad)])

    def swap_rows(block, parts):
        parts = parts if rows % (16 * parts) == 0 else 1
        return [from_mate(part, 1) for part in jnp.split(block, parts, axis=0)]

    fars, pieces, keeps, gots = [], [], [], []
    send_far(0)
    send_far(1)
    last = len(cols) - 1
    for i in range(len(cols)):
        seen = keeps[-1:]
        if i == last:
            x_mine, x_theirs = turn(order, after(x_own, keeps[-1]), x_nb, rows)
            x_rows = jnp.concatenate([x_mine, from_mate(x_theirs, 1)], axis=1)
        if i == last:
            seen += gots[:1] + [partner_weight]
        parts = SWAP_PARTS if i == last else 1
        far_mates = [p for w in fars[i] for p in swap_rows(after(w, *seen) if seen else w, parts)]
        pieces.append([slices[i], mates[i]] + fars[i] + far_mates)
        kept, given = forward_part(place, x_own, x_nb, pieces[i], scale, GIVE_PARTS)
        keeps += kept
        gots += [from_mate(give, 2) for give in given]
        if i + 2 <= last:
            send_far(i + 2)

    keeps[0] = after(keeps[0], partner_moment, x_rows)
    widths = [width for _, width in chunks(BWD_PARTS, features)]
    count = len(widths)
    cots = list(norm_cot(residual_in, upstream, norm_gain, keeps, gots, widths))

    half = rows // 2
    nbs = [from_mate(cot, 2) for cot in cots]
    mates = [from_mate(cot, 1) for cot in cots]
    kept, got, ours, theirs = [], [], [], []

    def gather(i):
        both = kept[i] + got[i].astype(F32)
        total = both[:half]
        for d in range(1, n_quad):
            total += shift_far(both[d * half : (d + 1) * half].astype(BF), d).astype(F32)
        ours.append(total)
        theirs.append(from_partner(total.astype(BF)))

    far_sums = []

    def sum_far(i):
        both = kept[i] + got[i].astype(F32)
        far_sums.append(
            [shift_far(both[d * half : (d + 1) * half].astype(BF), d) for d in range(1, n_quad)]
        )
        ours.append(both[:half])

    made, first_made, ig_own = [], [], []

    def give_back(i):
        total = ours[i]
        for block in far_sums[i]:
            total += block.astype(F32)
        if i == 1:
            total = after(total, ig_own[0])
        if i == count - 1:
            total = after(total, first_made[0])
        ours[i] = total
        theirs.append(from_partner(total.astype(BF)))

    def finish(i):
        start = chunks(BWD_PARTS, features)[i][0]
        made[:] = update(
            side.reshape(1).astype(jnp.int32),
            weight,
            partner_weight,
            momentum,
            partner_moment,
            ours[i],
            theirs[i],
            start,
            made,
        )
        first_made.append(made[0])

    nb_mates = [from_mate(nb, 1) for nb in nbs]
    for i in range(count + 2):
        if i < count:
            seen = kept[-1:]
            if i == 1:
                seen += nb_mates[2:]
            if i == 2:
                seen += [ig_nb]
            x_seen = after(x_rows, *seen) if seen else x_rows
            keep, give = gradient_part(x_seen, [cots[i], nbs[i], mates[i], nb_mates[i]], scale)
            kept.append(keep)
            got.append(from_partner(after(give, *got[-1:]) if got else give))
            if i == 1:
                first_nb = after(nbs[0], keep)
                ig_nb = input_grad_part(place, [first_nb] + nbs[1:], pieces, scale)
                ig_got = from_mate(ig_nb, 2)
            if i == 2:
                first_cot = after(cots[0], kept[-1])
                ig_own.append(input_grad_part(place, [first_cot] + cots[1:], pieces, scale))
        if 0 <= i - 2:
            give_back(i - 2)
            if i - 2 < count - 1:
                finish(i - 2)
        if 0 <= i - 1 < count:
            sum_far(i - 1)

    input_grad = interleave(near.reshape(1).astype(jnp.int32), after(ig_own[0], *made), ig_got, n_quad)

    finish(count - 1)
    new_weight, new_momentum = made
    return (input_grad, new_weight, new_momentum)


def solution(mesh):
    return jax.shard_map(
        per_device,
        mesh=mesh,
        in_specs=(
            P(("rep", "fsdp"), None),
            P(("rep", "fsdp"), None),
            P(("rep", "fsdp"), None),
            P(),
            P("rep", "fsdp", None),
            P("rep", "fsdp", None),
        ),
        out_specs=(P(("rep", "fsdp"), None), P("rep", "fsdp", None), P("rep", "fsdp", None)),
        check_vma=False,
    )
```
